32 devices in a mesh: blk: 8 (over z, y), col: 4 (over x, core).
Axes of the slice: x: 2, y: 2, z: 4, core: 2. Of those that a mesh axis runs over, the one named last changes fastest.
Arguments:
- amps: bfloat16 [8, 4, 2, 128, 128], P('blk', 'col'), may hold values from -6 to 6
- driver: float32 [8, 4, 2, 128, 128], P('blk', 'col')
- pattern: int32 [8, 4, 2, 8, 2], P('blk', 'col'), may hold values from -1 to 7, as said below
- domain: int32 [8, 4, 2], P('blk', 'col'), may hold values from 32 to 128
- virt_energy: float32 [8, 4, 2, 128], P('blk', 'col'), may hold values from 0.5 to 4
- pair_gap: float32 [8, 4, 2], P('blk', 'col'), may hold values from 0.5 to 2
- integrals: bfloat16 [8, 128, 128], P('col'), may hold values from -0.125 to 0.125
Outputs:
- new_amps: float32 [8, 4, 2, 128, 128], P('blk', 'col')
- resid_rms: float32 [], replicated
The draws below stay inside these ranges and needn't reach their ends.
Inputs may be any that keep to these rules, and one draw needn't show every extreme that they name: `pattern`: about a third of the entries are -1; the others name integral tiles of all owners.
All inputs are finite; a program needn't handle non-finite values.
Results may differ from the reference program's by a relative error of at most 0.0003.
Values may be sent and summed in bfloat16 or wider, within the bound.
No kernel may reach another device: no remote copies, remote signals or barrier semaphores. Data moves between devices by JAX's collectives and lax.ppermute only.
A program may use at most 64 MiB of HBM per device.

```python
import math
import jax
import jax.numpy as jnp
from jax import lax

V = 128
PD = 2
INT_DEV = 2
BLOCKS = 8
GROUPS = 4
NINT = 8


def draw_pattern(key, part):
    shape = (BLOCKS, GROUPS, PD, BLOCKS, PD)
    first, second = jax.random.split(key)
    tile_index = jax.random.randint(first, shape, 0, INT_DEV * GROUPS)
    keeper = jax.random.randint(second, shape, 0, 3)
    return jnp.where(keeper > 0, tile_index, -1).astype(jnp.int32)


def draw_driver(key, part):
    shape = (BLOCKS, GROUPS, PD, V, V)
    first = jax.random.fold_in(key, 0)
    place = (jnp.arange(BLOCKS)[:, None] * GROUPS + jnp.arange(GROUPS)[None, :]).astype(jnp.float32)
    place = place / float(max(BLOCKS * GROUPS - 1, 1))
    ramp = 0.5 + 1.5 * place
    base = jax.random.normal(first, shape, jnp.float32)
    return base * ramp[:, :, None, None, None]


def place_ends(entries, own_key, smallest, high):
    extent = entries.shape
    index_at = [jax.random.randint(jax.random.fold_in(own_key, axis), (), 0, extent[axis]) for axis in range(len(extent))]
    entries = entries.at[tuple(index_at)].set(smallest)
    longest = extent.index(max(extent))
    index_at[longest] = (index_at[longest] + 1) % extent[longest]
    return entries.at[tuple(index_at)].set(high)


def level_of(rng, dims, cuts, smallest, largest):
    gain = 1.0
    for dim, shards_of in cuts:
        heights = jax.random.uniform(jax.random.fold_in(jax.random.fold_in(rng, 6), dim), (shards_of,), jnp.float32, smallest / len(cuts), largest / len(cuts))
        gain = gain * jnp.repeat(jnp.exp(heights), dims[dim] // shards_of).reshape((-1,) + (1,) * (len(dims) - 1 - dim))
    return gain


def noise(rng, dims, scale, most, pieces=(), held_as=jnp.bfloat16):
    gain = level_of(rng, dims, pieces, -0.22, 0.18) if pieces else 1.0
    values = jax.random.normal(rng, dims, jnp.float32) * scale * gain
    return jnp.minimum(jnp.maximum(values, -most), most).astype(held_as)


def setup_inputs(seed: int = 0) -> dict:
    key_list = jax.random.split(jax.random.key(seed), 8)
    amps = noise(key_list[0], (BLOCKS, GROUPS, PD, V, V), 1.0, 6.0, ((0, 8), (1, 4)))
    driver = draw_driver(jax.random.fold_in(key_list[7], 71), 0)
    pattern = draw_pattern(jax.random.fold_in(key_list[7], 71), 0)
    domain = place_ends(jax.random.randint(key_list[3], (BLOCKS, GROUPS, PD), V // 4, V + 1), jax.random.fold_in(key_list[3], 1), V // 4, V).astype(jnp.int32)
    virt_energy = jnp.clip(jnp.exp(math.log(4.0) - 2.0794415 * jax.random.uniform(key_list[4], (BLOCKS, GROUPS, PD, V), jnp.float32) ** level_of(key_list[4], (BLOCKS, GROUPS, PD, V), ((0, 8), (1, 4)), -0.2, 0.2)), 0.5, 4.0)
    pair_gap = jnp.clip(jnp.exp(math.log(2.0) - 1.3862944 * jax.random.uniform(key_list[5], (BLOCKS, GROUPS, PD), jnp.float32) ** level_of(key_list[5], (BLOCKS, GROUPS, PD), ((0, 8), (1, 4)), -0.2, 0.2)), 0.5, 2.0)
    integrals = noise(key_list[6], (NINT, V, V), (V * BLOCKS * PD) ** -0.5, 0.125, ((0, 4),))
    return dict(amps=amps, driver=driver, pattern=pattern, domain=domain, virt_energy=virt_energy, pair_gap=pair_gap, integrals=integrals)


def reference(amps, driver, pattern, domain, virt_energy, pair_gap, integrals):
    width = amps.shape[-1]
    nblk = amps.shape[0]
    rows = jnp.arange(width, dtype=jnp.int32)
    edge = (rows < domain[..., None]).astype(jnp.float32)
    mask = edge[..., :, None] * edge[..., None, :]
    held = amps.astype(jnp.float32) * mask
    tiles_all = integrals.astype(jnp.float32)

    def one_block(index):
        links = pattern[index]

        def step(total, source):
            visit = held[source]
            idx = links[:, :, source, :]
            valid = (idx >= 0).astype(jnp.float32)
            tiles = tiles_all[jnp.maximum(idx, 0)] * valid[..., None, None]
            add = jnp.einsum('gqab,gpqbc->gpac', visit, tiles, precision=lax.Precision.HIGHEST)
            return (total + add, None)
        start = jnp.zeros(held.shape[1:], jnp.float32)
        total, _ = lax.scan(step, start, jnp.arange(nblk, dtype=jnp.int32))
        return total
    coupled = lax.map(one_block, jnp.arange(nblk, dtype=jnp.int32))
    resid = mask * (driver + coupled)
    denom = virt_energy[..., :, None] + virt_energy[..., None, :] + pair_gap[..., None, None]
    new_amps = held + resid / denom
    resid_rms = jnp.sqrt(jnp.sum(resid * resid) / float(resid.size))
    return (new_amps, resid_rms)
```

```python
import jax
import jax.numpy as jnp
from jax import lax
from jax.experimental import pallas as pl
from jax.experimental.pallas import tpu as pltpu
from jax.sharding import PartitionSpec as P

VMEM = pltpu.VMEM
SMEM = pltpu.SMEM


def edges(size, limit):
    rows = lax.broadcasted_iota(jnp.int32, (size, size), 0)
    cols = lax.broadcasted_iota(jnp.int32, (size, size), 1)
    return (rows < limit) & (cols < limit)


def hold_kernel(domain, amps, held):
    for p in range(amps.shape[0]):
        inside = edges(amps.shape[-1], domain[p])
        held[p] = jnp.where(inside, amps[p].astype(jnp.float32), 0.0).astype(held.dtype)


def couple_kernel(links, domain, gap, visits, table, driver, energy, energy_t, held, new, squares):
    pairs, width = held.shape[0], held.shape[-1]
    sources, per_source = visits.shape[0], visits.shape[1]
    acc = None

    def tile(p, t):
        k = links[p, t]
        block = table[jnp.maximum(k, 0)]
        return jnp.where(k >= 0, block, jnp.zeros_like(block))

    for s in range(sources):
        left = jnp.concatenate([visits[s, q] for q in range(per_source)], axis=1)
        right = jnp.concatenate(
            [
                jnp.concatenate([tile(p, s * per_source + q) for p in range(pairs)], axis=1)
                for q in range(per_source)
            ],
            axis=0,
        )
        part = jnp.dot(left, right, preferred_element_type=jnp.float32)
        acc = part if acc is None else acc + part
    total = jnp.zeros((1, width), jnp.float32)
    for p in range(pairs):
        inside = edges(width, domain[p])
        resid = jnp.where(inside, driver[p] + acc[:, p * width:(p + 1) * width], 0.0)
        denom = energy_t[:, p:p + 1] + energy[p:p + 1, :] + gap[p]
        new[p] = held[p].astype(jnp.float32) + resid / denom
        total = total + jnp.sum(resid * resid, axis=0, keepdims=True)
    squares[...] = jnp.broadcast_to(total, squares.shape)


def per_device(amps, driver, pattern, domain, virt_energy, pair_gap, integrals):
    pairs, width = amps.shape[2], amps.shape[-1]
    blocks, groups = lax.axis_size("blk"), lax.axis_size("col")
    links = pattern[0, 0].reshape(pairs, -1)
    spec = lambda space: pl.BlockSpec(memory_space=space)
    held = pl.pallas_call(
        hold_kernel,
        out_shape=jax.ShapeDtypeStruct((pairs, width, width), jnp.bfloat16),
        in_specs=[spec(SMEM), spec(VMEM)],
        out_specs=spec(VMEM),
    )(domain[0, 0], amps[0, 0])
    visits = lax.all_to_all(jnp.broadcast_to(held[None], (blocks,) + held.shape), "blk", 0, 0)
    table = lax.all_gather(integrals, "col", axis=0, tiled=True)
    energy = virt_energy[0, 0]
    new, squares = pl.pallas_call(
        couple_kernel,
        out_shape=[
            jax.ShapeDtypeStruct((pairs, width, width), jnp.float32),
            jax.ShapeDtypeStruct((blocks * groups, width), jnp.float32),
        ],
        in_specs=[spec(SMEM)] * 3 + [spec(VMEM)] * 6,
        out_specs=[spec(VMEM)] * 2,
    )(links, domain[0, 0], pair_gap[0, 0], visits, table, driver[0, 0], energy, energy.T, held)
    everyone = lax.all_to_all(squares, ("blk", "col"), 0, 0, tiled=True)
    entries = float(blocks * groups * pairs * width * width)
    resid_rms = jnp.sqrt(jnp.sum(everyone) / entries)
    return (new[None, None], resid_rms)


def solution(mesh):
    in_specs = (
        P("blk", "col", None, None, None),
        P("blk", "col", None, None, None),
        P("blk", "col", None, None, None),
        P("blk", "col", None),
        P("blk", "col", None, None),
        P("blk", "col", None),
        P("col", None, None),
    )
    out_specs = (P("blk", "col", None, None, None), P())
    return jax.shard_map(
        per_device, mesh=mesh, in_specs=in_specs, out_specs=out_specs, check_vma=False
    )
```

```python
import functools

import jax
import jax.numpy as jnp
from jax import lax
from jax.experimental import pallas as pl
from jax.experimental.pallas import tpu as pltpu
from jax.sharding import PartitionSpec as P

HBM = pltpu.HBM
VMEM = pltpu.VMEM
SMEM = pltpu.SMEM
LIMIT = 8 << 20


def edges(size, limit):
    rows = lax.broadcasted_iota(jnp.int32, (size, size), 0)
    cols = lax.broadcasted_iota(jnp.int32, (size, size), 1)
    return (rows < limit) & (cols < limit)


def hold_kernel(domain_in, amps_in, held, domain, amps, sem):
    copies = [
        pltpu.make_async_copy(domain_in, domain, sem.at[0]),
        pltpu.make_async_copy(amps_in, amps, sem.at[1]),
    ]
    for copy in copies:
        copy.start()
    for copy in copies:
        copy.wait()
    for p in range(amps.shape[0]):
        inside = edges(amps.shape[-1], domain[p])
        held[p] = jnp.where(inside, amps[p].astype(jnp.float32), 0.0).astype(held.dtype)


def product(left, right):
    return jnp.dot(left, right, preferred_element_type=jnp.float32)


def visits_of(ref, j, pairs):
    return jnp.concatenate([ref[j * pairs + q] for q in range(pairs)], axis=1)


def early_kernel(voffs, loffs, toffs, place, ring, links_in, domain_in, gap_in, driver_in, energy_in, *rest):
    visits = rest[:len(voffs)]
    tables = rest[len(voffs):len(voffs) + len(toffs)]
    weights, base, mask, inverse = rest[len(voffs) + len(toffs):][:4]
    table, links, domain, gap, driver, energy, sem = rest[len(voffs) + len(toffs) + 4:]
    small = [
        pltpu.make_async_copy(src, dst, sem.at[i])
        for i, (src, dst) in enumerate(
            [(links_in, links), (domain_in, domain), (gap_in, gap), (driver_in, driver), (energy_in, energy)]
        )
    ]
    for copy in small:
        copy.start()
    pairs, width = base.shape[0], base.shape[-1]
    count = table.shape[0] - 1
    table[count] = jnp.zeros((width, width), table.dtype)
    for offs, ref in zip(toffs, tables):
        own = ref.shape[0] // len(offs)
        for j, off in enumerate(offs):
            table[pl.ds((ring[0] ^ off) * own, own)] = ref[j * own:(j + 1) * own]
    for copy in small:
        copy.wait()

    def tile(p, s, q):
        k = links[p, q, s]
        return table[jnp.where(k < 0, count, k)]

    def weight(off):
        src = place[0] ^ off
        return jnp.concatenate(
            [
                jnp.concatenate([tile(p, src, q) for p in range(pairs)], axis=1)
                for q in range(pairs)
            ],
            axis=0,
        )

    acc = None
    for offs, ref in zip(voffs, visits):
        for j, off in enumerate(offs):
            part = product(visits_of(ref, j, pairs), weight(off))
            acc = part if acc is None else acc + part
    for i, off in enumerate(loffs):
        weights[i] = weight(off)
    for p in range(pairs):
        inside = edges(width, domain[p])
        base[p] = jnp.where(inside, driver[p] + acc[:, p * width:(p + 1) * width], 0.0)
        mask[p] = inside.astype(jnp.float32)
        along = jnp.broadcast_to(energy[p:p + 1, :], (width, width))
        inverse[p] = 1.0 / (along.T + along + gap[p])


def late_kernel(counts, held, weights, base, mask, inverse, *rest):
    visits = rest[:len(counts)]
    new, squares = rest[len(counts):]
    pairs, width = base.shape[0], base.shape[-1]
    acc = None
    i = 0
    for n, ref in zip(counts, visits):
        for j in range(n):
            part = product(visits_of(ref, j, pairs), weights[i])
            acc = part if acc is None else acc + part
            i += 1
    total = jnp.zeros((1, width), jnp.float32)
    for p in range(pairs):
        resid = base[p] + mask[p] * acc[:, p * width:(p + 1) * width]
        new[p] = held[p].astype(jnp.float32) + resid * inverse[p]
        total = total + jnp.sum(resid * resid, axis=0, keepdims=True)
    squares[...] = jnp.broadcast_to(total, squares.shape)


def finish_kernel(entries, rows, out):
    total = jnp.sum(rows[...], axis=0, keepdims=True)
    total = jnp.sum(total, axis=1, keepdims=True)
    out[...] = jnp.sqrt(total / entries)


def xor(v, axis, k):
    return lax.ppermute(v, axis, [(i, i ^ k) for i in range(lax.axis_size(axis))])


def spread(own, axis, steps):
    have = {(0,): own}
    for k, pieces in steps:
        if pieces in have:
            v = have[pieces]
        else:
            v = jnp.concatenate([have[(i,)] for i in pieces], 0)
        have[tuple(i ^ k for i in pieces)] = xor(v, axis, k)
    return list(have.items())


def block_steps(size):
    far = list(range(size - 2, 2, -2))
    steps = [(k, (0,)) for k in far[1:]] + [(1, (0,))] + [(k, (0,)) for k in far[:1]]
    steps += [(2, (0, 1))] if size > 2 else []
    far.reverse()
    return steps + [(1, tuple(far[i:i + 2])) for i in range(0, len(far), 2)]


def tile_steps(size):
    far = tuple(range(2, size, 2))
    return [(k, (0,)) for k in far] + [(1, (0,) + far)]


def put(x, space):
    return pltpu.with_memory_space_constraint(x, space)


def spec(space):
    return pl.BlockSpec(memory_space=space)


def per_device(amps, driver, pattern, domain, virt_energy, pair_gap, integrals):
    pairs, width = amps.shape[2], amps.shape[-1]
    blocks, groups = lax.axis_size("blk"), lax.axis_size("col")
    count = groups * integrals.shape[0]
    links = pattern[0, 0].transpose(0, 2, 1)
    params = pltpu.CompilerParams(vmem_limit_bytes=LIMIT)
    DMA = pltpu.SemaphoreType.DMA
    tile = (pairs, width, width)
    held = pl.pallas_call(
        hold_kernel,
        out_shape=VMEM(tile, jnp.bfloat16),
        in_specs=[spec(HBM)] * 2,
        out_specs=spec(VMEM),
        scratch_shapes=[SMEM((pairs,), jnp.int32), VMEM(tile, jnp.bfloat16), DMA((2,))],
        compiler_params=params,
    )(put(domain[0, 0], HBM), put(amps[0, 0], HBM))
    pieces = spread(held, "blk", block_steps(blocks))
    tables = spread(integrals, "col", tile_steps(groups))
    early, late = pieces[:-1], pieces[-1:]
    place = lax.axis_index("blk").reshape(1)
    ring = lax.axis_index("col").reshape(1)
    loffs = [off for offs, _ in late for off in offs]
    args = [links, domain[0, 0], pair_gap[0, 0], driver[0, 0], virt_energy[0, 0]]
    big = [v for _, v in early] + [v for _, v in tables]
    weights, base, mask, inverse = pl.pallas_call(
        functools.partial(early_kernel, [o for o, _ in early], loffs, [o for o, _ in tables]),
        out_shape=[VMEM((len(loffs), pairs * width, pairs * width), jnp.bfloat16)] + [VMEM(tile, jnp.float32)] * 3,
        in_specs=[spec(SMEM)] * 2 + [spec(HBM)] * 5 + [spec(VMEM)] * len(big),
        out_specs=[spec(VMEM)] * 4,
        scratch_shapes=[
            VMEM((count + 1, width, width), jnp.bfloat16),
            SMEM(links.shape, jnp.int32),
            SMEM((pairs,), jnp.int32),
            SMEM((pairs,), jnp.float32),
            VMEM(tile, jnp.float32),
            VMEM((pairs, width), jnp.float32),
            DMA((5,)),
        ],
        compiler_params=params,
    )(place, ring, *[put(v, HBM) for v in args], *[put(v, VMEM) for v in big])
    new, squares = pl.pallas_call(
        functools.partial(late_kernel, [len(o) for o, _ in late]),
        out_shape=[
            VMEM(tile, jnp.float32),
            VMEM((blocks * groups, width), jnp.float32),
        ],
        in_specs=[spec(VMEM)] * (5 + len(late)),
        out_specs=[spec(VMEM)] * 2,
        compiler_params=params,
    )(*[put(v, VMEM) for v in (held, weights, base, mask, inverse)], *[put(v, VMEM) for _, v in late])
    entries = float(blocks * groups * pairs * width * width)
    rows = lax.all_to_all(squares, ("blk", "col"), 0, 0, tiled=True)
    rms = pl.pallas_call(
        functools.partial(finish_kernel, entries),
        out_shape=jax.ShapeDtypeStruct((1, 1), jnp.float32),
        in_specs=[spec(VMEM)],
        out_specs=spec(VMEM),
        compiler_params=params,
    )(put(rows, VMEM))
    return (new[None, None], rms.reshape(()))


def solution(mesh):
    in_specs = (
        P("blk", "col", None, None, None),
        P("blk", "col", None, None, None),
        P("blk", "col", None, None, None),
        P("blk", "col", None),
        P("blk", "col", None, None),
        P("blk", "col", None),
        P("col", None, None),
    )
    out_specs = (P("blk", "col", None, None, None), P())
    return jax.shard_map(
        per_device, mesh=mesh, in_specs=in_specs, out_specs=out_specs, check_vma=False
    )
```

```python
import functools

import jax
import jax.numpy as jnp
from jax import lax
from jax.experimental import pallas as pl
from jax.experimental.pallas import tpu as pltpu
from jax.sharding import PartitionSpec as P

HBM = pltpu.HBM
VMEM = pltpu.VMEM
SMEM = pltpu.SMEM
LIMIT = 8 << 20
NEWV = True


def edges(size, limit):
    rows = lax.broadcasted_iota(jnp.int32, (size, size), 0)
    cols = lax.broadcasted_iota(jnp.int32, (size, size), 1)
    return (rows < limit) & (cols < limit)


def hold_kernel(domain_in, amps_in, held, domain, amps, sem):
    copies = [
        pltpu.make_async_copy(domain_in, domain, sem.at[0]),
        pltpu.make_async_copy(amps_in, amps, sem.at[1]),
    ]
    for copy in copies:
        copy.start()
    for copy in copies:
        copy.wait()
    for p in range(amps.shape[0]):
        inside = edges(amps.shape[-1], domain[p])
        held[p] = jnp.where(inside, amps[p].astype(jnp.float32), 0.0).astype(held.dtype)


def product(left, right):
    return jnp.dot(left, right, preferred_element_type=jnp.float32)


def visits_of(ref, j, pairs):
    return jnp.concatenate([ref[j * pairs + q] for q in range(pairs)], axis=1)


def early_kernel(voffs, loffs, toffs, place, ring, links_in, domain_in, gap_in, driver_in, energy_in, own_in, *rest):
    visits = rest[:len(voffs)]
    tables = rest[len(voffs):len(voffs) + len(toffs)]
    weights, base, mask, inverse = rest[len(voffs) + len(toffs):][:4]
    table, links, domain, gap, driver, energy, sem = rest[len(voffs) + len(toffs) + 4:]
    small = [
        pltpu.make_async_copy(src, dst, sem.at[i])
        for i, (src, dst) in enumerate(
            [(links_in, links), (domain_in, domain), (gap_in, gap), (driver_in, driver), (energy_in, energy)]
        )
    ]
    pairs, width = base.shape[0], base.shape[-1]
    count = table.shape[0] - 1
    own = own_in.shape[0]
    small.append(pltpu.make_async_copy(own_in, table.at[pl.ds(ring[0] * own, own)], sem.at[5]))
    for copy in small:
        copy.start()
    table[count] = jnp.zeros((width, width), table.dtype)
    for offs, ref in zip(toffs, tables):
        for j, off in enumerate(offs):
            table[pl.ds((ring[0] ^ off) * own, own)] = ref[j * own:(j + 1) * own]
    for copy in small:
        copy.wait()

    def tile(p, s, q):
        k = links[p, q, s]
        return table[jnp.where(k < 0, count, k)]

    def weight(off):
        src = place[0] ^ off
        return jnp.concatenate(
            [
                jnp.concatenate([tile(p, src, q) for p in range(pairs)], axis=1)
                for q in range(pairs)
            ],
            axis=0,
        )

    acc = None
    for offs, ref in zip(voffs, visits):
        for j, off in enumerate(offs):
            part = product(visits_of(ref, j, pairs), weight(off))
            acc = part if acc is None else acc + part
    for i, off in enumerate(loffs):
        block = weight(off)
        weights[i * block.shape[0]:(i + 1) * block.shape[0]] = block
    for p in range(pairs):
        inside = edges(width, domain[p])
        base[p] = jnp.where(inside, driver[p] + acc[:, p * width:(p + 1) * width], 0.0)
        mask[p] = inside.astype(jnp.float32)
        along = jnp.broadcast_to(energy[p:p + 1, :], (width, width))
        inverse[p] = 1.0 / (along.T + along + gap[p])


def late_kernel(counts, weights, base, mask, *rest):
    visits, (resid, squares) = rest[:len(counts)], rest[len(counts):]
    pairs, width = base.shape[0], base.shape[-1]
    left = jnp.concatenate([visits_of(ref, j, pairs) for n, ref in zip(counts, visits) for j in range(n)], axis=1)
    acc = product(left, weights[...])
    total = jnp.zeros((1, width), jnp.float32)
    for p in range(pairs):
        value = base[p] + mask[p] * acc[:, p * width:(p + 1) * width]
        resid[p] = value
        total = total + jnp.sum(value * value, axis=0, keepdims=True)
    squares[...] = jnp.broadcast_to(total, squares.shape)


def finish_kernel(entries, rows, held, resid, inverse, new, rms):
    new[...] = held[...].astype(jnp.float32) + resid[...] * inverse[...]
    total = jnp.sum(rows[...], axis=0, keepdims=True)
    total = jnp.sum(total, axis=1, keepdims=True)
    rms[...] = jnp.sqrt(total / entries)


def xor(v, axis, k):
    return lax.ppermute(v, axis, [(i, i ^ k) for i in range(lax.axis_size(axis))])


def spread(own, axis, steps):
    have, single, n = {(0,): own}, {0: own}, own.shape[0]
    for k, pieces in steps:
        if pieces in have:
            v = have[pieces]
        else:
            v = jnp.concatenate([single[i] for i in pieces], 0) if len(pieces) > 1 else single[pieces[0]]
        got = xor(v, axis, k)
        offs = tuple(i ^ k for i in pieces)
        have[offs] = got
        for j, i in enumerate(offs):
            single[i] = got[j * n:(j + 1) * n] if len(offs) > 1 else got
    return list(have.items())


def block_steps(size):
    far = list(range(size - 2, 2, -2))
    steps = [(k, (0,)) for k in far[1:]] + [(1, (0,))] + [(k, (0,)) for k in far[:1]]
    steps += [(2, (0, 1))] if size > 2 else []
    far.reverse()
    return steps + [(1, tuple(far[i:i + 2])) for i in range(0, len(far), 2)]


def tile_steps(size):
    far = range(2, size, 2)
    return [(k, (0,)) for k in far] + [(1, (0,))] + [(1, (k,)) for k in far]


def put(x, space):
    return pltpu.with_memory_space_constraint(x, space)


def spec(space):
    return pl.BlockSpec(memory_space=space)


def per_device(amps, driver, pattern, domain, virt_energy, pair_gap, integrals):
    pairs, width = amps.shape[2], amps.shape[-1]
    blocks, groups = lax.axis_size("blk"), lax.axis_size("col")
    count = groups * integrals.shape[0]
    links = pattern[0, 0].transpose(0, 2, 1)
    params = pltpu.CompilerParams(vmem_limit_bytes=LIMIT)
    DMA = pltpu.SemaphoreType.DMA
    tile = (pairs, width, width)
    tables = spread(integrals, "col", tile_steps(groups))
    held = pl.pallas_call(
        hold_kernel,
        out_shape=VMEM(tile, jnp.bfloat16),
        in_specs=[spec(HBM)] * 2,
        out_specs=spec(VMEM),
        scratch_shapes=[SMEM((pairs,), jnp.int32), VMEM(tile, jnp.bfloat16), DMA((2,))],
        compiler_params=params,
    )(put(domain[0, 0], HBM), put(amps[0, 0], HBM))
    pieces = spread(held, "blk", block_steps(blocks))
    early, late = pieces[:-1], pieces[-1:]
    place = lax.axis_index("blk").reshape(1)
    ring = lax.axis_index("col").reshape(1)
    loffs = [off for offs, _ in late for off in offs]
    args = [links, domain[0, 0], pair_gap[0, 0], driver[0, 0], virt_energy[0, 0], integrals]
    tables = tables[1:]
    big = [v for _, v in early] + [v for _, v in tables]
    weights, base, mask, inverse = pl.pallas_call(
        functools.partial(early_kernel, [o for o, _ in early], loffs, [o for o, _ in tables]),
        out_shape=[VMEM((len(loffs) * pairs * width, pairs * width), jnp.bfloat16)] + [VMEM(tile, jnp.float32)] * 3,
        in_specs=[spec(SMEM)] * 2 + [spec(HBM)] * 6 + [spec(VMEM)] * len(big),
        out_specs=[spec(VMEM)] * 4,
        scratch_shapes=[
            VMEM((count + 1, width, width), jnp.bfloat16),
            SMEM(links.shape, jnp.int32),
            SMEM((pairs,), jnp.int32),
            SMEM((pairs,), jnp.float32),
            VMEM(tile, jnp.float32),
            VMEM((pairs, width), jnp.float32),
            DMA((6,)),
        ],
        compiler_params=params,
    )(place, ring, *[put(v, HBM) for v in args], *[put(v, VMEM) for v in big])
    resid, squares = pl.pallas_call(
        functools.partial(late_kernel, [len(o) for o, _ in late]),
        out_shape=[VMEM(tile, jnp.float32), VMEM((blocks * groups, width), jnp.float32)],
        in_specs=[spec(VMEM)] * (3 + len(late)),
        out_specs=[spec(VMEM)] * 2,
        compiler_params=params,
    )(*[put(v, VMEM) for v in (weights, base, mask)], *[put(v, VMEM) for _, v in late])
    entries = float(blocks * groups * pairs * width * width)
    rows = lax.all_to_all(squares, ("blk", "col"), 0, 0, tiled=True)
    new, rms = pl.pallas_call(
        functools.partial(finish_kernel, entries),
        out_shape=[jax.ShapeDtypeStruct(tile, jnp.float32), jax.ShapeDtypeStruct((1, 1), jnp.float32)],
        in_specs=[spec(VMEM)] * 4,
        out_specs=[spec(VMEM)] * 2,
        compiler_params=params,
    )(*[put(v, VMEM) for v in (rows, held, resid, inverse)])
    return (new[None, None], rms.reshape(()))


def solution(mesh):
    in_specs = (
        P("blk", "col", None, None, None),
        P("blk", "col", None, None, None),
        P("blk", "col", None, None, None),
        P("blk", "col", None),
        P("blk", "col", None, None),
        P("blk", "col", None),
        P("col", None, None),
    )
    out_specs = (P("blk", "col", None, None, None), P())
    return jax.shard_map(
        per_device, mesh=mesh, in_specs=in_specs, out_specs=out_specs, check_vma=False
    )
```

```python
import functools

import jax
import jax.numpy as jnp
from jax import lax
from jax.experimental import pallas as pl
from jax.experimental.pallas import tpu as pltpu
from jax.sharding import PartitionSpec as P

HBM = pltpu.HBM
VMEM = pltpu.VMEM
SMEM = pltpu.SMEM
LIMIT = 8 << 20
NEWV = True


def edges(size, limit):
    rows = lax.broadcasted_iota(jnp.int32, (size, size), 0)
    cols = lax.broadcasted_iota(jnp.int32, (size, size), 1)
    return (rows < limit) & (cols < limit)


def hold_kernel(domain_in, amps_in, held, domain, amps, sem):
    copies = [
        pltpu.make_async_copy(domain_in, domain, sem.at[0]),
        pltpu.make_async_copy(amps_in, amps, sem.at[1]),
    ]
    for copy in copies:
        copy.start()
    for copy in copies:
        copy.wait()
    for p in range(amps.shape[0]):
        inside = edges(amps.shape[-1], domain[p])
        held[p] = jnp.where(inside, amps[p].astype(jnp.float32), 0.0).astype(held.dtype)


def product(left, right):
    return jnp.dot(left, right, preferred_element_type=jnp.float32)


def visits_of(ref, j, pairs):
    return jnp.concatenate([ref[j * pairs + q] for q in range(pairs)], axis=1)


def early_kernel(voffs, loffs, toffs, place, ring, links_in, domain_in, gap_in, driver_in, energy_in, own_in, *rest):
    visits = rest[:len(voffs)]
    tables = rest[len(voffs):len(voffs) + len(toffs)]
    weights, base, mask, inverse = rest[len(voffs) + len(toffs):][:4]
    table, links, domain, gap, driver, energy, sem = rest[len(voffs) + len(toffs) + 4:]
    small = [
        pltpu.make_async_copy(src, dst, sem.at[i])
        for i, (src, dst) in enumerate(
            [(links_in, links), (domain_in, domain), (gap_in, gap), (driver_in, driver), (energy_in, energy)]
        )
    ]
    pairs, width = base.shape[0], base.shape[-1]
    count = table.shape[0] - 1
    own = own_in.shape[0]
    small.append(pltpu.make_async_copy(own_in, table.at[pl.ds(ring[0] * own, own)], sem.at[5]))
    for copy in small:
        copy.start()
    table[count] = jnp.zeros((width, width), table.dtype)
    for offs, ref in zip(toffs, tables):
        for j, off in enumerate(offs):
            table[pl.ds((ring[0] ^ off) * own, own)] = ref[j * own:(j + 1) * own]
    for copy in small:
        copy.wait()

    def tile(p, s, q):
        k = links[p, q, s]
        return table[jnp.where(k < 0, count, k)]

    def weight(off):
        src = place[0] ^ off
        return jnp.concatenate(
            [
                jnp.concatenate([tile(p, src, q) for p in range(pairs)], axis=1)
                for q in range(pairs)
            ],
            axis=0,
        )

    acc = None
    for offs, ref in zip(voffs, visits):
        for j, off in enumerate(offs):
            part = product(visits_of(ref, j, pairs), weight(off))
            acc = part if acc is None else acc + part
    for i, off in enumerate(loffs):
        block = weight(off)
        weights[i * block.shape[0]:(i + 1) * block.shape[0]] = block
    for p in range(pairs):
        inside = edges(width, domain[p])
        base[p] = jnp.where(inside, driver[p] + acc[:, p * width:(p + 1) * width], 0.0)
        mask[p] = inside.astype(jnp.float32)
        along = jnp.broadcast_to(energy[p:p + 1, :], (width, width))
        inverse[p] = 1.0 / (along.T + along + gap[p])


def late_kernel(counts, weights, base, mask, *rest):
    visits, (resid, squares) = rest[:len(counts)], rest[len(counts):]
    pairs, width = base.shape[0], base.shape[-1]
    left = jnp.concatenate([visits_of(ref, j, pairs) for n, ref in zip(counts, visits) for j in range(n)], axis=1)
    acc = product(left, weights[...])
    total = jnp.zeros((1, width), jnp.float32)
    for p in range(pairs):
        value = base[p] + mask[p] * acc[:, p * width:(p + 1) * width]
        resid[p] = value
        total = total + jnp.sum(value * value, axis=0, keepdims=True)
    squares[...] = jnp.broadcast_to(total, squares.shape)


def finish_kernel(entries, rows, held, resid, inverse, new, rms):
    new[...] = held[...].astype(jnp.float32) + resid[...] * inverse[...]
    total = jnp.sum(rows[...], axis=0, keepdims=True)
    total = jnp.sum(total, axis=1, keepdims=True)
    rms[...] = jnp.sqrt(total / entries)


def xor(v, axis, k):
    return lax.ppermute(v, axis, [(i, i ^ k) for i in range(lax.axis_size(axis))])


def spread(own, axis, steps):
    have, single, n = {(0,): own}, {0: own}, own.shape[0]
    for k, pieces in steps:
        if pieces in have:
            v = have[pieces]
        else:
            v = jnp.concatenate([single[i] for i in pieces], 0) if len(pieces) > 1 else single[pieces[0]]
        got = xor(v, axis, k)
        offs = tuple(i ^ k for i in pieces)
        have[offs] = got
        for j, i in enumerate(offs):
            single[i] = got[j * n:(j + 1) * n] if len(offs) > 1 else got
    return list(have.items())


def block_steps(size):
    far = tuple(range(4, size, 4))
    first = [(1, (0,))] + [(k, (0,)) for k in far]
    last = [(2, (0, 1))] if size > 2 else []
    if far:
        last += [(k, far) for k in (1, 2, 3)]
    return first, last


def tile_steps(size):
    far = range(2, size, 2)
    return [(k, (0,)) for k in far] + [(1, (0,))] + [(1, (k,)) for k in far]


def put(x, space):
    return pltpu.with_memory_space_constraint(x, space)


def spec(space):
    return pl.BlockSpec(memory_space=space)


def per_device(amps, driver, pattern, domain, virt_energy, pair_gap, integrals):
    pairs, width = amps.shape[2], amps.shape[-1]
    blocks, groups = lax.axis_size("blk"), lax.axis_size("col")
    count = groups * integrals.shape[0]
    links = pattern[0, 0].transpose(0, 2, 1)
    params = pltpu.CompilerParams(vmem_limit_bytes=LIMIT)
    DMA = pltpu.SemaphoreType.DMA
    tile = (pairs, width, width)
    held = pl.pallas_call(
        hold_kernel,
        out_shape=VMEM(tile, jnp.bfloat16),
        in_specs=[spec(HBM)] * 2,
        out_specs=spec(VMEM),
        scratch_shapes=[SMEM((pairs,), jnp.int32), VMEM(tile, jnp.bfloat16), DMA((2,))],
        compiler_params=params,
    )(put(domain[0, 0], HBM), put(amps[0, 0], HBM))
    tables = spread(integrals, "col", tile_steps(groups))
    first, last = block_steps(blocks)
    pieces = spread(held, "blk", first + last)
    ahead = len(pieces) - max(len(last), 1)
    early, late = pieces[:ahead], pieces[ahead:]
    late = late[-1:] + late[1:-1] + late[:1] if len(late) > 1 else late
    place = lax.axis_index("blk").reshape(1)
    ring = lax.axis_index("col").reshape(1)
    loffs = [off for offs, _ in late for off in offs]
    args = [links, domain[0, 0], pair_gap[0, 0], driver[0, 0], virt_energy[0, 0], integrals]
    tables = tables[1:]
    big = [v for _, v in early] + [v for _, v in tables]
    weights, base, mask, inverse = pl.pallas_call(
        functools.partial(early_kernel, [o for o, _ in early], loffs, [o for o, _ in tables]),
        out_shape=[VMEM((len(loffs) * pairs * width, pairs * width), jnp.bfloat16)] + [VMEM(tile, jnp.float32)] * 3,
        in_specs=[spec(SMEM)] * 2 + [spec(HBM)] * 6 + [spec(VMEM)] * len(big),
        out_specs=[spec(VMEM)] * 4,
        scratch_shapes=[
            VMEM((count + 1, width, width), jnp.bfloat16),
            SMEM(links.shape, jnp.int32),
            SMEM((pairs,), jnp.int32),
            SMEM((pairs,), jnp.float32),
            VMEM(tile, jnp.float32),
            VMEM((pairs, width), jnp.float32),
            DMA((6,)),
        ],
        compiler_params=params,
    )(place, ring, *[put(v, HBM) for v in args], *[put(v, VMEM) for v in big])
    resid, squares = pl.pallas_call(
        functools.partial(late_kernel, [len(o) for o, _ in late]),
        out_shape=[VMEM(tile, jnp.float32), VMEM((blocks * groups, width), jnp.float32)],
        in_specs=[spec(VMEM)] * (3 + len(late)),
        out_specs=[spec(VMEM)] * 2,
        compiler_params=params,
    )(*[put(v, VMEM) for v in (weights, base, mask)], *[put(v, VMEM) for _, v in late])
    entries = float(blocks * groups * pairs * width * width)
    rows = lax.all_to_all(squares, ("blk", "col"), 0, 0, tiled=True)
    new, rms = pl.pallas_call(
        functools.partial(finish_kernel, entries),
        out_shape=[jax.ShapeDtypeStruct(tile, jnp.float32), jax.ShapeDtypeStruct((1, 1), jnp.float32)],
        in_specs=[spec(VMEM)] * 4,
        out_specs=[spec(VMEM)] * 2,
        compiler_params=params,
    )(*[put(v, VMEM) for v in (rows, held, resid, inverse)])
    return (new[None, None], rms.reshape(()))


def solution(mesh):
    in_specs = (
        P("blk", "col", None, None, None),
        P("blk", "col", None, None, None),
        P("blk", "col", None, None, None),
        P("blk", "col", None),
        P("blk", "col", None, None),
        P("blk", "col", None),
        P("col", None, None),
    )
    out_specs = (P("blk", "col", None, None, None), P())
    return jax.shard_map(
        per_device, mesh=mesh, in_specs=in_specs, out_specs=out_specs, check_vma=False
    )
```

```python
import functools

import jax
import jax.numpy as jnp
from jax import lax
from jax.experimental import pallas as pl
from jax.experimental.pallas import tpu as pltpu
from jax.sharding import PartitionSpec as P

HBM = pltpu.HBM
VMEM = pltpu.VMEM
SMEM = pltpu.SMEM
LIMIT = 8 << 20
NEWV = True


def edges(size, limit):
    rows = lax.broadcasted_iota(jnp.int32, (size, size), 0)
    cols = lax.broadcasted_iota(jnp.int32, (size, size), 1)
    return (rows < limit) & (cols < limit)


def hold_kernel(domain_in, amps_in, held, domain, amps, sem):
    pairs = amps.shape[0]
    copies = [pltpu.make_async_copy(amps_in.at[p], amps.at[p], sem.at[p]) for p in range(pairs)]
    limit = pltpu.make_async_copy(domain_in, domain, sem.at[pairs])
    limit.start()
    for copy in copies:
        copy.start()
    limit.wait()
    for p in range(pairs):
        inside = edges(amps.shape[-1], domain[p])
        copies[p].wait()
        held[p] = jnp.where(inside, amps[p].astype(jnp.float32), 0.0).astype(held.dtype)


def product(left, right):
    return jnp.dot(left, right, preferred_element_type=jnp.float32)


def visits_of(ref, j, pairs):
    return jnp.concatenate([ref[j * pairs + q] for q in range(pairs)], axis=1)


def early_kernel(voffs, loffs, toffs, place, ring, links_in, domain_in, gap_in, driver_in, energy_in, own_in, *rest):
    visits = rest[:len(voffs)]
    tables = rest[len(voffs):len(voffs) + len(toffs)]
    weights, base, mask, inverse = rest[len(voffs) + len(toffs):][:4]
    table, links, domain, gap, driver, energy, sem = rest[len(voffs) + len(toffs) + 4:]
    small = [
        pltpu.make_async_copy(src, dst, sem.at[i])
        for i, (src, dst) in enumerate(
            [(links_in, links), (domain_in, domain), (gap_in, gap), (driver_in, driver), (energy_in, energy)]
        )
    ]
    pairs, width = base.shape[0], base.shape[-1]
    count = table.shape[0] - 1
    own = own_in.shape[0]
    small.append(pltpu.make_async_copy(own_in, table.at[pl.ds(ring[0] * own, own)], sem.at[5]))
    for copy in small:
        copy.start()
    table[count] = jnp.zeros((width, width), table.dtype)
    for offs, ref in zip(toffs, tables):
        for j, off in enumerate(offs):
            table[pl.ds((ring[0] ^ off) * own, own)] = ref[j * own:(j + 1) * own]
    for copy in small:
        copy.wait()

    def tile(p, s, q):
        k = links[p, q, s]
        return table[jnp.where(k < 0, count, k)]

    def weight(off):
        src = place[0] ^ off
        return jnp.concatenate(
            [
                jnp.concatenate([tile(p, src, q) for p in range(pairs)], axis=1)
                for q in range(pairs)
            ],
            axis=0,
        )

    acc = None
    for offs, ref in zip(voffs, visits):
        for j, off in enumerate(offs):
            part = product(visits_of(ref, j, pairs), weight(off))
            acc = part if acc is None else acc + part
    for i, off in enumerate(loffs):
        block = weight(off)
        weights[i * block.shape[0]:(i + 1) * block.shape[0]] = block
    for p in range(pairs):
        inside = edges(width, domain[p])
        base[p] = jnp.where(inside, driver[p] + acc[:, p * width:(p + 1) * width], 0.0)
        mask[p] = inside.astype(jnp.float32)
        along = jnp.broadcast_to(energy[p:p + 1, :], (width, width))
        inverse[p] = 1.0 / (along.T + along + gap[p])


def late_kernel(counts, weights, base, mask, *rest):
    visits, (resid, squares) = rest[:len(counts)], rest[len(counts):]
    pairs, width = base.shape[0], base.shape[-1]
    left = jnp.concatenate([visits_of(ref, j, pairs) for n, ref in zip(counts, visits) for j in range(n)], axis=1)
    acc = product(left, weights[...])
    total = jnp.zeros((1, width), jnp.float32)
    for p in range(pairs):
        value = base[p] + mask[p] * acc[:, p * width:(p + 1) * width]
        resid[p] = value
        total = total + jnp.sum(value * value, axis=0, keepdims=True)
    squares[...] = jnp.broadcast_to(total, squares.shape)


def finish_kernel(entries, rows, held, resid, inverse, new, rms):
    new[...] = held[...].astype(jnp.float32) + resid[...] * inverse[...]
    total = jnp.sum(rows[...], axis=0, keepdims=True)
    total = jnp.sum(total, axis=1, keepdims=True)
    rms[...] = jnp.sqrt(total / entries)


def xor(v, axis, k):
    return lax.ppermute(v, axis, [(i, i ^ k) for i in range(lax.axis_size(axis))])


def spread(own, axis, steps):
    have, single, n = {(0,): own}, {0: own}, own.shape[0]
    for k, pieces in steps:
        if pieces in have:
            v = have[pieces]
        else:
            v = jnp.concatenate([single[i] for i in pieces], 0) if len(pieces) > 1 else single[pieces[0]]
        got = xor(v, axis, k)
        offs = tuple(i ^ k for i in pieces)
        have[offs] = got
        for j, i in enumerate(offs):
            single[i] = got[j * n:(j + 1) * n] if len(offs) > 1 else got
    return list(have.items())


def block_steps(size):
    far = tuple(range(4, size, 4))
    first = [(1, (0,))] + [(k, (0,)) for k in far]
    last = [(2, (0, 1))] if size > 2 else []
    if far:
        last += [(k, far) for k in (1, 2, 3)]
    return first, last


def tile_steps(size):
    far = range(2, size, 2)
    return [(1, (0,))] + [(k + 1, (0,)) for k in far] + [(k, (0,)) for k in far]


def put(x, space):
    return pltpu.with_memory_space_constraint(x, space)


def spec(space):
    return pl.BlockSpec(memory_space=space)


def per_device(amps, driver, pattern, domain, virt_energy, pair_gap, integrals):
    pairs, width = amps.shape[2], amps.shape[-1]
    blocks, groups = lax.axis_size("blk"), lax.axis_size("col")
    count = groups * integrals.shape[0]
    links = pattern[0, 0].transpose(0, 2, 1)
    params = pltpu.CompilerParams(vmem_limit_bytes=LIMIT)
    DMA = pltpu.SemaphoreType.DMA
    tile = (pairs, width, width)
    held = pl.pallas_call(
        hold_kernel,
        out_shape=VMEM(tile, jnp.bfloat16),
        in_specs=[spec(HBM)] * 2,
        out_specs=spec(VMEM),
        scratch_shapes=[SMEM((pairs,), jnp.int32), VMEM(tile, jnp.bfloat16), DMA((pairs + 1,))],
        compiler_params=params,
    )(put(domain[0, 0], HBM), put(amps[0, 0], HBM))
    tables = spread(integrals, "col", tile_steps(groups))
    first, last = block_steps(blocks)
    pieces = spread(held, "blk", first + last)
    ahead = len(pieces) - max(len(last), 1)
    early, late = pieces[:ahead], pieces[ahead:]
    late = late[-1:] + late[1:-1] + late[:1] if len(late) > 1 else late
    place = lax.axis_index("blk").reshape(1)
    ring = lax.axis_index("col").reshape(1)
    loffs = [off for offs, _ in late for off in offs]
    args = [links, domain[0, 0], pair_gap[0, 0], driver[0, 0], virt_energy[0, 0], integrals]
    tables = tables[1:]
    big = [v for _, v in early] + [v for _, v in tables]
    weights, base, mask, inverse = pl.pallas_call(
        functools.partial(early_kernel, [o for o, _ in early], loffs, [o for o, _ in tables]),
        out_shape=[VMEM((len(loffs) * pairs * width, pairs * width), jnp.bfloat16)] + [VMEM(tile, jnp.float32)] * 3,
        in_specs=[spec(SMEM)] * 2 + [spec(HBM)] * 6 + [spec(VMEM)] * len(big),
        out_specs=[spec(VMEM)] * 4,
        scratch_shapes=[
            VMEM((count + 1, width, width), jnp.bfloat16),
            SMEM(links.shape, jnp.int32),
            SMEM((pairs,), jnp.int32),
            SMEM((pairs,), jnp.float32),
            VMEM(tile, jnp.float32),
            VMEM((pairs, width), jnp.float32),
            DMA((6,)),
        ],
        compiler_params=params,
    )(place, ring, *[put(v, HBM) for v in args], *[put(v, VMEM) for v in big])
    resid, squares = pl.pallas_call(
        functools.partial(late_kernel, [len(o) for o, _ in late]),
        out_shape=[VMEM(tile, jnp.float32), VMEM((blocks * groups, width), jnp.float32)],
        in_specs=[spec(VMEM)] * (3 + len(late)),
        out_specs=[spec(VMEM)] * 2,
        compiler_params=params,
    )(*[put(v, VMEM) for v in (weights, base, mask)], *[put(v, VMEM) for _, v in late])
    entries = float(blocks * groups * pairs * width * width)
    rows = lax.all_to_all(squares, ("blk", "col"), 0, 0, tiled=True)
    new, rms = pl.pallas_call(
        functools.partial(finish_kernel, entries),
        out_shape=[jax.ShapeDtypeStruct(tile, jnp.float32), jax.ShapeDtypeStruct((1, 1), jnp.float32)],
        in_specs=[spec(VMEM)] * 4,
        out_specs=[spec(VMEM)] * 2,
        compiler_params=params,
    )(*[put(v, VMEM) for v in (rows, held, resid, inverse)])
    return (new[None, None], rms.reshape(()))


def solution(mesh):
    in_specs = (
        P("blk", "col", None, None, None),
        P("blk", "col", None, None, None),
        P("blk", "col", None, None, None),
        P("blk", "col", None),
        P("blk", "col", None, None),
        P("blk", "col", None),
        P("col", None, None),
    )
    out_specs = (P("blk", "col", None, None, None), P())
    return jax.shard_map(
        per_device, mesh=mesh, in_specs=in_specs, out_specs=out_specs, check_vma=False
    )
```

```python
import functools

import jax
import jax.numpy as jnp
from jax import lax
from jax.experimental import pallas as pl
from jax.experimental.pallas import tpu as pltpu
from jax.sharding import PartitionSpec as P

HBM = pltpu.HBM
VMEM = pltpu.VMEM
SMEM = pltpu.SMEM
LIMIT = 8 << 20
NEWV = True


def edges(size, limit):
    rows = lax.broadcasted_iota(jnp.int32, (size, size), 0)
    cols = lax.broadcasted_iota(jnp.int32, (size, size), 1)
    return (rows < limit) & (cols < limit)


def hold_kernel(domain_in, amps_in, held, domain, amps, sem):
    pairs = amps.shape[0]
    copies = [pltpu.make_async_copy(amps_in.at[p], amps.at[p], sem.at[p]) for p in range(pairs)]
    limit = pltpu.make_async_copy(domain_in, domain, sem.at[pairs])
    limit.start()
    for copy in copies:
        copy.start()
    limit.wait()
    for p in range(pairs):
        inside = edges(amps.shape[-1], domain[p])
        copies[p].wait()
        held[p] = jnp.where(inside, amps[p].astype(jnp.float32), 0.0).astype(held.dtype)


def product(left, right):
    return jnp.dot(left, right, preferred_element_type=jnp.float32)


def visits_of(ref, j, pairs):
    return jnp.concatenate([ref[j * pairs + q] for q in range(pairs)], axis=1)


def early_kernel(voffs, loffs, toffs, place, ring, links_in, domain_in, gap_in, driver_in, energy_in, own_in, *rest):
    visits = rest[:len(voffs)]
    tables = rest[len(voffs):len(voffs) + len(toffs)]
    weights, base, mask, inverse = rest[len(voffs) + len(toffs):][:4]
    table, links, domain, gap, driver, energy, sem = rest[len(voffs) + len(toffs) + 4:]
    small = [
        pltpu.make_async_copy(src, dst, sem.at[i])
        for i, (src, dst) in enumerate(
            [(links_in, links), (domain_in, domain), (gap_in, gap), (driver_in, driver), (energy_in, energy)]
        )
    ]
    pairs, width = base.shape[0], base.shape[-1]
    count = table.shape[0] - 1
    own = own_in.shape[0]
    small.append(pltpu.make_async_copy(own_in, table.at[pl.ds(ring[0] * own, own)], sem.at[5]))
    for copy in small:
        copy.start()
    table[count] = jnp.zeros((width, width), table.dtype)
    for offs, ref in zip(toffs, tables):
        for j, off in enumerate(offs):
            table[pl.ds((ring[0] ^ off) * own, own)] = ref[j * own:(j + 1) * own]
    for copy in small:
        copy.wait()

    def tile(p, s, q):
        k = links[p, q, s]
        return table[jnp.where(k < 0, count, k)]

    def weight(off):
        src = place[0] ^ off
        return jnp.concatenate(
            [
                jnp.concatenate([tile(p, src, q) for p in range(pairs)], axis=1)
                for q in range(pairs)
            ],
            axis=0,
        )

    acc = None
    for offs, ref in zip(voffs, visits):
        for j, off in enumerate(offs):
            part = product(visits_of(ref, j, pairs), weight(off))
            acc = part if acc is None else acc + part
    for i, off in enumerate(loffs):
        block = weight(off)
        weights[i * block.shape[0]:(i + 1) * block.shape[0]] = block
    for p in range(pairs):
        inside = edges(width, domain[p])
        base[p] = jnp.where(inside, driver[p] + acc[:, p * width:(p + 1) * width], 0.0)
        mask[p] = inside.astype(jnp.float32)
        along = jnp.broadcast_to(energy[p:p + 1, :], (width, width))
        inverse[p] = 1.0 / (along.T + along + gap[p])


def late_kernel(counts, weights, base, mask, *rest):
    visits, (resid, squares) = rest[:len(counts)], rest[len(counts):]
    pairs, width = base.shape[0], base.shape[-1]
    left = jnp.concatenate([visits_of(ref, j, pairs) for n, ref in zip(counts, visits) for j in range(n)], axis=1)
    acc = product(left, weights[...])
    total = jnp.zeros((1, width), jnp.float32)
    for p in range(pairs):
        value = base[p] + mask[p] * acc[:, p * width:(p + 1) * width]
        resid[p] = value
        total = total + jnp.sum(value * value, axis=0, keepdims=True)
    squares[...] = jnp.broadcast_to(total, squares.shape)


def finish_kernel(entries, rows, held, resid, inverse, new_out, rms, new, sem):
    copies = []
    for p in range(new.shape[0]):
        new[p] = held[p].astype(jnp.float32) + resid[p] * inverse[p]
        copies.append(pltpu.make_async_copy(new.at[p], new_out.at[p], sem.at[p]))
        copies[p].start()
    total = jnp.sum(rows[...], axis=0, keepdims=True)
    total = jnp.sum(total, axis=1, keepdims=True)
    rms[...] = jnp.sqrt(total / entries)
    for copy in copies:
        copy.wait()


def xor(v, axis, k):
    return lax.ppermute(v, axis, [(i, i ^ k) for i in range(lax.axis_size(axis))])


def spread(own, axis, steps):
    have, single, n = {(0,): own}, {0: own}, own.shape[0]
    for k, pieces in steps:
        if pieces in have:
            v = have[pieces]
        else:
            v = jnp.concatenate([single[i] for i in pieces], 0) if len(pieces) > 1 else single[pieces[0]]
        got = xor(v, axis, k)
        offs = tuple(i ^ k for i in pieces)
        have[offs] = got
        for j, i in enumerate(offs):
            single[i] = got[j * n:(j + 1) * n] if len(offs) > 1 else got
    return list(have.items())


def block_steps(size):
    far = tuple(range(4, size, 4))
    first = [(1, (0,))] + [(k, (0,)) for k in far]
    last = [(2, (0, 1))] if size > 2 else []
    if far:
        last += [(k, far) for k in (1, 2, 3)]
    return first, last


def tile_steps(size):
    far = range(2, size, 2)
    return [(1, (0,))] + [(k + 1, (0,)) for k in far] + [(k, (0,)) for k in far]


def put(x, space):
    return pltpu.with_memory_space_constraint(x, space)


def spec(space):
    return pl.BlockSpec(memory_space=space)


def per_device(amps, driver, pattern, domain, virt_energy, pair_gap, integrals):
    pairs, width = amps.shape[2], amps.shape[-1]
    blocks, groups = lax.axis_size("blk"), lax.axis_size("col")
    count = groups * integrals.shape[0]
    links = pattern[0, 0].transpose(0, 2, 1)
    params = pltpu.CompilerParams(vmem_limit_bytes=LIMIT)
    DMA = pltpu.SemaphoreType.DMA
    tile = (pairs, width, width)
    held = pl.pallas_call(
        hold_kernel,
        out_shape=VMEM(tile, jnp.bfloat16),
        in_specs=[spec(HBM)] * 2,
        out_specs=spec(VMEM),
        scratch_shapes=[SMEM((pairs,), jnp.int32), VMEM(tile, jnp.bfloat16), DMA((pairs + 1,))],
        compiler_params=params,
    )(put(domain[0, 0], HBM), put(amps[0, 0], HBM))
    tables = spread(integrals, "col", tile_steps(groups))
    first, last = block_steps(blocks)
    pieces = spread(held, "blk", first + last)
    ahead = len(pieces) - max(len(last), 1)
    early, late = pieces[:ahead], pieces[ahead:]
    late = late[-1:] + late[1:-1] + late[:1] if len(late) > 1 else late
    place = lax.axis_index("blk").reshape(1)
    ring = lax.axis_index("col").reshape(1)
    loffs = [off for offs, _ in late for off in offs]
    args = [links, domain[0, 0], pair_gap[0, 0], driver[0, 0], virt_energy[0, 0], integrals]
    tables = tables[1:]
    big = [v for _, v in early] + [v for _, v in tables]
    weights, base, mask, inverse = pl.pallas_call(
        functools.partial(early_kernel, [o for o, _ in early], loffs, [o for o, _ in tables]),
        out_shape=[VMEM((len(loffs) * pairs * width, pairs * width), jnp.bfloat16)] + [VMEM(tile, jnp.float32)] * 3,
        in_specs=[spec(SMEM)] * 2 + [spec(HBM)] * 6 + [spec(VMEM)] * len(big),
        out_specs=[spec(VMEM)] * 4,
        scratch_shapes=[
            VMEM((count + 1, width, width), jnp.bfloat16),
            SMEM(links.shape, jnp.int32),
            SMEM((pairs,), jnp.int32),
            SMEM((pairs,), jnp.float32),
            VMEM(tile, jnp.float32),
            VMEM((pairs, width), jnp.float32),
            DMA((6,)),
        ],
        compiler_params=params,
    )(place, ring, *[put(v, HBM) for v in args], *[put(v, VMEM) for v in big])
    resid, squares = pl.pallas_call(
        functools.partial(late_kernel, [len(o) for o, _ in late]),
        out_shape=[VMEM(tile, jnp.float32), VMEM((blocks * groups, width), jnp.float32)],
        in_specs=[spec(VMEM)] * (3 + len(late)),
        out_specs=[spec(VMEM)] * 2,
        compiler_params=params,
    )(*[put(v, VMEM) for v in (weights, base, mask)], *[put(v, VMEM) for _, v in late])
    entries = float(blocks * groups * pairs * width * width)
    rows = lax.all_to_all(squares, ("blk", "col"), 0, 0, tiled=True)
    new, rms = pl.pallas_call(
        functools.partial(finish_kernel, entries),
        out_shape=[jax.ShapeDtypeStruct(tile, jnp.float32), jax.ShapeDtypeStruct((1, 1), jnp.float32)],
        in_specs=[spec(VMEM)] * 4,
        out_specs=[spec(HBM), spec(VMEM)],
        scratch_shapes=[VMEM(tile, jnp.float32), DMA((pairs,))],
        compiler_params=params,
    )(*[put(v, VMEM) for v in (rows, held, resid, inverse)])
    return (new[None, None], rms.reshape(()))


def solution(mesh):
    in_specs = (
        P("blk", "col", None, None, None),
        P("blk", "col", None, None, None),
        P("blk", "col", None, None, None),
        P("blk", "col", None),
        P("blk", "col", None, None),
        P("blk", "col", None),
        P("col", None, None),
    )
    out_specs = (P("blk", "col", None, None, None), P())
    return jax.shard_map(
        per_device, mesh=mesh, in_specs=in_specs, out_specs=out_specs, check_vma=False
    )
```
